32 devices in a mesh: lhs: 8 (over y, x, core), rhs: 4 (over z).
Axes of the slice: x: 2, y: 2, z: 4, core: 2. Of those that a mesh axis runs over, the one named last changes fastest.
Arguments:
- left_table: float32 [8, 4, 384, 400], P('lhs', 'rhs'), may hold values from -6 to 6
- left_state: float32 [8, 4, 384], P('lhs', 'rhs'), may hold values from 1e-06 to 0.0001
- right_table: float32 [8, 4, 384, 400], P('lhs', 'rhs'), may hold values from -6 to 6
- right_state: float32 [8, 4, 384], P('lhs', 'rhs'), may hold values from 1e-06 to 0.0001
- operators: float32 [2, 400, 400], replicated, may hold values from -0.3125 to 0.3125
- operator_state: float32 [2, 400], replicated, may hold values from 0.1 to 10
- sources: int32 [8, 4, 384], P('lhs', 'rhs'), may hold values from 0 to 383
- targets: int32 [8, 4, 384], P('lhs', 'rhs'), may hold values from 0 to 383
- relations: int32 [8, 4, 384], P('lhs', 'rhs'), may hold values from 0 to 1, as said below
- negatives: int32 [8, 4, 384], P('lhs', 'rhs'), may hold values from 0 to 383
- counts: int32 [8, 4], P('lhs', 'rhs'), may hold values from 1 to 384, 960 in all within a row
Outputs:
- new_left: float32 [8, 4, 384, 400], P('lhs', 'rhs')
- new_right: float32 [8, 4, 384, 400], P('lhs', 'rhs')
- new_operators: float32 [2, 400, 400], replicated
The draws below stay inside these ranges and needn't reach their ends.
Inputs may be any that keep to these rules, and one draw needn't show every extreme that they name: For each index along lhs, the counts over rhs sum to 960, and at least one of them equals 384. `relations`: within each bucket the edge slots are grouped by relation: relation ids never fall from one slot to the next.
All inputs are finite; a program needn't handle non-finite values. No bound on the sum of `counts` on one device may be relied on, other than what follows from the above.
Results may differ from the reference program's by a relative error of at most 0.0003.
Values sent between devices are 32-bit elements; how exact they have to be, the bound alone decides.
No kernel may reach another device: no remote copies, remote signals or barrier semaphores. Data moves between devices by JAX's collectives and lax.ppermute only.
A program may use at most 64 MiB of HBM per device.

```python
import math
import jax
import jax.numpy as jnp
import numpy as np
from jax import lax

WIDTH = 400
RELATION_TYPES = 2
SAMPLES = 384
ROWS = 384
EDGES = 384
BUCKET_TOTAL = 960
N_LHS = 8
N_RHS = 4


def draw_relations(key, part):
    key = jax.random.fold_in(key, 7)
    split_at = jax.random.randint(key, (N_LHS, N_RHS, 1), 0, EDGES + 1)
    slots = jnp.arange(EDGES, dtype=jnp.int32)
    return (slots[None, None, :] >= split_at).astype(jnp.int32)


def touch_ends(values, stream_key, low, top_value):
    shape = values.shape
    place = [jax.random.randint(jax.random.fold_in(stream_key, axis), (), 0, shape[axis]) for axis in range(len(shape))]
    values = values.at[tuple(place)].set(low)
    longest = shape.index(max(shape))
    place[longest] = (place[longest] + 1) % shape[longest]
    return values.at[tuple(place)].set(top_value)


def block_levels(key, extent, split, low, largest):
    def one(dim, shards_of):
        heights = jax.random.uniform(jax.random.fold_in(jax.random.fold_in(key, 6), dim), (shards_of,), jnp.float32, low / len(split), largest / len(split))
        return jnp.repeat(jnp.exp(heights), extent[dim] // shards_of).reshape((-1,) + (1,) * (len(extent) - dim - 1))

    gain = one(*split[0])
    for cut in split[1:]:
        gain = gain * one(*cut)
    return gain


def split_up(amount, total, most, lean):
    portions = [(1 << 20) // math.isqrt(standing ** lean) + 1 for standing in range(2, amount + 1)]
    surplus, given = total - most - (amount - 1), [1] * (amount - 1)
    while surplus > 0:
        candidates = [i for i in range(amount - 1) if given[i] < most]
        whole, budget = sum([portions[i] for i in candidates]), surplus
        for i in candidates:
            extra = min(most - given[i], max(1, budget * portions[i] // whole), surplus)
            given[i] = given[i] + extra
            surplus = surplus - extra
    return np.array([most] + given)


def ragged(key, number_of, total, reach, skew):
    if number_of == 2:
        one = jax.random.randint(key, (), max(1, total - reach), min(reach, total - 1) + 1)
        return jnp.stack([one, total - one])
    tallies = jnp.asarray(split_up(number_of, total, reach, skew), jnp.int32)
    couples = (number_of - 1) // 2
    giver, sink = tallies[1:1 + 2 * couples:2], tallies[2:2 + 2 * couples:2]
    slack = jnp.minimum(giver - 1, reach - sink)
    passed = jax.random.randint(jax.random.fold_in(key, 1), (couples,), 0, 1 << 20) % (slack + 1)
    tallies = tallies.at[1:1 + 2 * couples:2].set(giver - passed).at[2:2 + 2 * couples:2].set(sink + passed)
    return tallies[jax.random.permutation(jax.random.fold_in(key, 2), number_of)]


def normal_values(rng, shape, deviation, bound, split=(), held_as=jnp.bfloat16):
    loudness = block_levels(rng, shape, split, -0.22, 0.18) if split else 1.0
    entries = jax.random.normal(rng, shape, jnp.float32) * deviation * loudness
    return jnp.minimum(jnp.maximum(entries, -bound), bound).astype(held_as)


def setup_inputs(seed: int = 0) -> dict:
    keys = jax.random.split(jax.random.key(seed), 12)
    return {
        "left_table": normal_values(keys[0], (N_LHS, N_RHS, ROWS, WIDTH), 1.0, 6.0, ((0, 8), (1, 4)), jnp.float32),
        "left_state": jnp.clip(jnp.exp(math.log(0.0001) - 4.6051702 * jax.random.uniform(keys[1], (N_LHS, N_RHS, ROWS), jnp.float32) ** block_levels(keys[1], (N_LHS, N_RHS, ROWS), ((0, 8), (1, 4)), -0.2, 0.2)), 9.999999974752427e-07, 0.0001),
        "right_table": normal_values(keys[2], (N_LHS, N_RHS, ROWS, WIDTH), 1.0, 6.0, ((0, 8), (1, 4)), jnp.float32),
        "right_state": jnp.clip(jnp.exp(math.log(0.0001) - 4.6051702 * jax.random.uniform(keys[3], (N_LHS, N_RHS, ROWS), jnp.float32) ** block_levels(keys[3], (N_LHS, N_RHS, ROWS), ((0, 8), (1, 4)), -0.2, 0.2)), 9.999999974752427e-07, 0.0001),
        "operators": normal_values(keys[4], (RELATION_TYPES, WIDTH, WIDTH), WIDTH ** -0.5, 0.3125, (), jnp.float32),
        "operator_state": jnp.clip(jnp.exp(jax.random.uniform(keys[5], (RELATION_TYPES, WIDTH), jnp.float32, math.log(0.1), math.log(10.0))), 0.1, 10.0),
        "sources": touch_ends(jax.random.randint(keys[6], (N_LHS, N_RHS, EDGES), 0, ROWS), jax.random.fold_in(keys[6], 1), 0, ROWS - 1).astype(jnp.int32),
        "targets": touch_ends(jax.random.randint(keys[7], (N_LHS, N_RHS, EDGES), 0, ROWS), jax.random.fold_in(keys[7], 1), 0, ROWS - 1).astype(jnp.int32),
        "relations": draw_relations(jax.random.fold_in(keys[11], 71), 0),
        "negatives": touch_ends(jax.random.randint(keys[9], (N_LHS, N_RHS, SAMPLES), 0, ROWS), jax.random.fold_in(keys[9], 1), 0, ROWS - 1).astype(jnp.int32),
        "counts": jax.vmap(lambda own: ragged(own, N_RHS, BUCKET_TOTAL, EDGES, 2))(jax.random.split(keys[10], N_LHS)).reshape((N_LHS, N_RHS)).astype(jnp.int32),
    }


def bucket_loss(left_block, right_block, operators, sources, targets, relations, negatives, live_count):
    inputs = left_block[sources]
    mapped_all = jnp.einsum('ew,rwv->erv', inputs, operators, precision=lax.Precision.HIGHEST)
    kind_ids = jnp.arange(operators.shape[0], dtype=jnp.int32)
    select = (relations[:, None] == kind_ids[None, :]).astype(jnp.float32)
    mapped = lax.optimization_barrier(jnp.sum(mapped_all * select[:, :, None], axis=1))
    unit_mapped = mapped * lax.rsqrt(lax.optimization_barrier(jnp.sum(mapped * mapped, -1, keepdims=True)) + 1e-06)
    unit_right = right_block * lax.rsqrt(lax.optimization_barrier(jnp.sum(right_block * right_block, -1, keepdims=True)) + 1e-06)
    positive = lax.optimization_barrier(jnp.sum(unit_mapped * unit_right[targets], -1))
    sampled = jnp.dot(unit_mapped, unit_right[negatives].T, precision=lax.Precision.HIGHEST)
    log_total = jnp.log(jnp.exp(positive) + lax.optimization_barrier(jnp.sum(jnp.exp(sampled), -1)))
    live_slot = jnp.arange(sources.shape[0], dtype=jnp.int32) < live_count
    return jnp.sum(jnp.where(live_slot, log_total - positive, jnp.zeros_like(log_total)))

def adagrad(weights, sums_in, gradient):
    summed = sums_in + lax.optimization_barrier(jnp.mean(gradient * gradient, -1))
    return weights - 0.1 * gradient / jnp.sqrt(summed)[..., None]

def reference(left_table, left_state, right_table, right_state, operators, operator_state, sources, targets, relations, negatives, counts):
    devices = N_LHS * N_RHS
    left_window = jnp.roll(left_table, 1, axis=0).reshape(devices, ROWS, WIDTH)
    left_wstate = jnp.roll(left_state, 1, axis=0).reshape(devices, ROWS)
    right_window = jnp.roll(right_table, 1, axis=1).reshape(devices, ROWS, WIDTH)
    right_wstate = jnp.roll(right_state, 1, axis=1).reshape(devices, ROWS)
    scan_items = (left_window, right_window, sources.reshape(devices, EDGES), targets.reshape(devices, EDGES), relations.reshape(devices, EDGES), negatives.reshape(devices, SAMPLES), counts.reshape(devices))

    def visit_bucket(summed, bucket_item):
        left_block, right_block, src_rows, dst_rows, kind_rows, neg_rows, live_count = bucket_item

        def local_loss(first, second, third):
            return bucket_loss(first, second, third, src_rows, dst_rows, kind_rows, neg_rows, live_count)
        loss_value, pullback = jax.vjp(local_loss, left_block, right_block, operators)
        left_grad, right_grad, operator_grad = pullback(jnp.ones_like(loss_value))
        return (summed + operator_grad, (left_grad, right_grad))
    operator_grad, row_grads = lax.scan(visit_bucket, jnp.zeros_like(operators), scan_items)
    new_left = adagrad(left_window, left_wstate, row_grads[0]).reshape(N_LHS, N_RHS, ROWS, WIDTH)
    new_right = adagrad(right_window, right_wstate, row_grads[1]).reshape(N_LHS, N_RHS, ROWS, WIDTH)
    new_operators = adagrad(operators, operator_state, operator_grad)
    return (new_left, new_right, new_operators)
```

```python
import functools

import jax
import jax.numpy as jnp
from jax import lax
from jax.experimental import pallas as pl
from jax.experimental.pallas import tpu as pltpu
from jax.sharding import PartitionSpec as P

F32 = jnp.float32
BF16 = jnp.bfloat16
LANES = 128
NN = ((1,), (0,))
NT = ((1,), (1,))
TN = ((0,), (0,))
EPS = 1e-06


def cut(x):
    high = x.astype(BF16)
    low = (x - high.astype(F32)).astype(BF16)
    return high, low


def mul(a, b, dims):
    return lax.dot_general(a, b, (dims, ((), ())), preferred_element_type=F32)


def mul3(a, b, dims):
    return mul(a[0], b[0], dims) + (mul(a[0], b[1], dims) + mul(a[1], b[0], dims))


def deep3(a, b, dims):
    (da,), (db,) = dims
    left = jnp.concatenate([a[0], a[0], a[1]], axis=da)
    right = jnp.concatenate([b[0], b[1], b[0]], axis=db)
    return mul(left, right, dims)


def one_hot(index_row, rows):
    shape = (rows, index_row.shape[1])
    return lax.broadcasted_iota(jnp.int32, shape, 0) == index_row


def prepare_kernel(
    count, src, tgt, neg, ops, op_sums,
    pick, weight, hit, live, column, ops_high, ops_low,
):
    rows, slots = pick.shape
    w = ops.shape[1]
    pick[...] = one_hot(src[...], rows).astype(BF16)
    target = jnp.transpose(one_hot(tgt[...], rows).astype(F32))
    sample = jnp.transpose(one_hot(neg[...], rows).astype(F32))
    alive = (lax.broadcasted_iota(jnp.int32, (slots, 1), 0) < count[0, 0]).astype(F32)
    weight[...] = target + jnp.sum(sample, axis=0, keepdims=True)
    hit[...] = target * alive
    live[...] = alive
    diagonal = one_hot(lax.broadcasted_iota(jnp.int32, (1, w), 1), w)
    for i in range(ops.shape[0]):
        column[i] = jnp.sum(jnp.where(diagonal, op_sums[i:i + 1, :], 0.0), axis=1, keepdims=True)
        high, low = cut(ops[i])
        ops_high[i] = high
        ops_low[i] = low


def left_kernel(after, left, ops_high, ops_low, pick, rel, x_high, x_low, unit, scale, turned_high, turned_low):
    high, low = cut(left[...])
    xh = mul(high, pick[...], NN).astype(BF16)
    xl = mul(low, pick[...], NN).astype(BF16)
    x_high[...] = xh
    x_low[...] = xl
    first = mul3((ops_high[0], ops_low[0]), (xh, xl), TN)
    second = mul3((ops_high[1], ops_low[1]), (xh, xl), TN)
    mapped = jnp.where(rel[...] == 0, first, second)
    inv = lax.rsqrt(jnp.sum(mapped * mapped, axis=0, keepdims=True) + EPS)
    u = mapped * inv
    unit[...] = u
    scale[...] = inv
    high, low = cut(jnp.transpose(u))
    turned_high[...] = high
    turned_low[...] = low


def operator_grad(which, relations, d_high, d_low, x, out):
    own = relations == which
    masked = [jnp.where(own, part.astype(F32), 0.0).astype(BF16) for part in (d_high, d_low)]
    grad = deep3(x, masked, NT)
    w = grad.shape[0]
    tiles, rest = w // LANES, w % LANES
    for t in range(tiles):
        out[pl.ds(t * w, w), :] = grad[:, t * LANES:(t + 1) * LANES]
    tail = jnp.transpose(grad[:, tiles * LANES:])
    base = tiles * w
    out[pl.ds(base, out.shape[0] - base), :] = jnp.zeros((out.shape[0] - base, LANES), F32)
    for t in range(-(-w // LANES)):
        width = min(LANES, w - t * LANES)
        out[pl.ds(base + t * rest, rest), 0:width] = tail[:, t * LANES:t * LANES + width]


def right_kernel(
    after, right, unit, scale, turned_high, turned_low, weight, hit, live, rel, x_high, x_low,
    send, d_high, d_low, p_high, p_low,
):
    r = right[...]
    split = cut(r)
    inv = lax.rsqrt(jnp.sum(r * r, axis=0, keepdims=True) + EPS)
    scores = mul3((turned_high[...], turned_low[...]), split, NN) * inv
    weighted = jnp.exp(scores) * weight[...]
    total = jnp.sum(weighted, axis=1, keepdims=True)
    push = weighted * (live[...] / total) - hit[...]
    p_high[...], p_low[...] = cut(push)
    du = deep3(split, cut(push * inv), NT)
    u = unit[...]
    along = jnp.sum(u * du, axis=0, keepdims=True)
    dh, dl = cut(scale[...] * (du - u * along))
    d_high[...] = dh
    d_low[...] = dl
    operator_grad(1 - core(), rel[...], dh, dl, (x_high[...], x_low[...]), send)


def keep_kernel(rel, d_high, d_low, x_high, x_low, keep):
    operator_grad(core(), rel[...], d_high[...], d_low[...], (x_high[...], x_low[...]), keep)


def adagrad_t(weights, sums, grad):
    summed = sums + jnp.sum(grad * grad, axis=0, keepdims=True) / grad.shape[0]
    return weights - grad * (0.1 / jnp.sqrt(summed))


def left_update_kernel(
    after, left, left_sum, ops_high, ops_low, pick, rel, d_high, d_low, new_left, done,
):
    d = (d_high[...], d_low[...])
    first = mul3((ops_high[0], ops_low[0]), d, NN)
    second = mul3((ops_high[1], ops_low[1]), d, NN)
    dx = cut(jnp.where(rel[...] == 0, first, second))
    grad = mul(dx[0], pick[...], NT) + mul(dx[1], pick[...], NT)
    new_left[...] = adagrad_t(left[...], left_sum[...], grad)
    done[...] = jnp.zeros_like(done)


def right_update_kernel(after, right, right_sum, unit, p_high, p_low, new_right, done):
    r = right[...]
    inv = lax.rsqrt(jnp.sum(r * r, axis=0, keepdims=True) + EPS)
    v = r * inv
    dv = deep3(cut(unit[...]), (p_high[...], p_low[...]), NN)
    grad = inv * (dv - v * jnp.sum(v * dv, axis=0, keepdims=True))
    new_right[...] = adagrad_t(r, right_sum[...], grad)
    done[...] = jnp.zeros_like(done)


def core():
    return lax.rem(lax.axis_index("lhs"), 2)


def chip():
    return lax.div(lax.axis_index("lhs"), 2)


def side():
    return lax.rem(lax.axis_index("rhs"), 2)


def deal_kernel(one, two, *outs):
    direct, distant = peers_of(one.shape[0])
    for half, own in enumerate((1 - side(), side())):
        own_outs = outs[half * (len(direct) + 1):]

        def part(j):
            spot = jnp.bitwise_xor(chip(), j)
            return one[spot, own] + two[spot, own]

        for j, out in zip(direct, own_outs):
            out[...] = part(j)
        for i, j in enumerate(distant):
            own_outs[len(direct)][i] = part(j)


def merge_kernel(one, two, *outs):
    for i, out in enumerate(outs):
        out[...] = one[i] + two[i]


def sum_kernel(*refs, after):
    refs = refs[after:]
    refs[-1][...] = functools.reduce(jnp.add, [ref[...] for ref in refs[:-1]])


def join_kernel(*refs):
    out = refs[-1]
    for j, ref in zip(walk_of(len(refs) - 1), refs):
        out[jnp.bitwise_xor(chip(), j)] = ref[...]


def copy_kernel(after, value, out):
    out[...] = value[...]


def operator_rows(which, ops, sums, near, far, flat, store):
    chunk = near.shape[1]
    for j in range(near.shape[0]):
        for own, ref in ((side(), near), (1 - side(), far)):
            flat[pl.ds(pl.multiple_of((2 * j + own) * chunk, 8), chunk), :] = ref[j]
    w = ops.shape[1]
    main = w // LANES
    rest = w - main * LANES
    tiles = [flat[pl.ds(t * w, w), :] for t in range(main)]
    tail = jnp.concatenate(
        [flat[pl.ds(main * w + t * rest, rest), :] for t in range(-(-w // LANES))], axis=1
    )
    tail = jnp.transpose(tail)[:w]
    square = jnp.sum(tail * tail, axis=1, keepdims=True)
    square = square + jnp.sum(sum(tile * tile for tile in tiles), axis=1, keepdims=True)
    rate = 0.1 / jnp.sqrt(sums[which] + square / w)
    for t, part in enumerate([*tiles, tail]):
        span = slice(t * LANES, min(w, (t + 1) * LANES))
        store(span, ops[which, :, span] - part * rate)


def own_operator_kernel(ops, sums, near, far, out, flat):
    def store(span, value):
        out[:, span] = value

    operator_rows(core(), ops, sums, near, far, flat, store)


def operator_kernel(own, ops, sums, near, far, out, flat, half, sem):
    first = pltpu.make_async_copy(own, out.at[core()], sem.at[0])
    first.start()

    def store(span, value):
        half[:, span] = value

    operator_rows(1 - core(), ops, sums, near, far, flat, store)
    second = pltpu.make_async_copy(half, out.at[1 - core()], sem.at[1])
    second.start()
    first.wait()
    second.wait()


def shaped(shape, dtype=F32):
    return jax.ShapeDtypeStruct(shape, dtype)


VMEM = pl.BlockSpec(memory_space=pltpu.VMEM)
ANY = pl.BlockSpec(memory_space=pl.ANY)
SMEM = pl.BlockSpec(memory_space=pltpu.SMEM)


def run(kernel, out_shape, scalars, *args, after=(), scratch=(), out_specs=None, flops=0, name=None):
    specs = [SMEM] * len(scalars) + [ANY] * len(after) + [VMEM] * len(args)
    return pl.pallas_call(
        kernel,
        out_shape=out_shape,
        in_specs=specs,
        out_specs=out_specs or jax.tree.map(lambda _: VMEM, out_shape),
        scratch_shapes=scratch,
        compiler_params=pltpu.CompilerParams(vmem_limit_bytes=24 * 2**20),
        cost_estimate=pl.CostEstimate(flops=flops, bytes_accessed=2**20, transcendentals=0),
        name=name,
    )(*scalars, *after, *args)


def around(value, axis, steps):
    count = lax.axis_size(axis)
    return lax.ppermute(value, axis, [(i, (i + steps) % count) for i in range(count)])


def swap(value, axis, bit):
    count = lax.axis_size(axis)
    return lax.ppermute(value, axis, [(i, i ^ bit) for i in range(count)])


def across_cores(value):
    return swap(value, "lhs", 1)


def peers_of(count):
    return [j for j in range(count) if j.bit_count() < 2], [j for j in range(count) if j.bit_count() > 1]


def walk_of(count):
    return [j ^ (j // 2) for j in range(count)]


def across_chips(value, j):
    return swap(value, "lhs", 2 * j)


def body(
    left_table, left_state, right_table, right_state, operators, operator_state,
    sources, targets, relations, negatives, counts,
):
    rows, w = left_table.shape[2:]
    slots = sources.shape[2]
    chips = lax.axis_size("lhs") // 2
    layers = lax.axis_size("rhs")
    unit_rows = 16 * chips
    used = w // LANES * w + (w % LANES) * -(-w // LANES)
    packed = -(-used // unit_rows) * unit_rows

    right = around(jnp.swapaxes(right_table[0, 0], 0, 1), "rhs", 1)
    left = around(jnp.swapaxes(left_table[0, 0], 0, 1), "lhs", 1)
    left_sum = around(left_state[0], "lhs", 1)
    right_sum = around(right_state[0], "rhs", 1)
    rel = relations[0]
    wide = shaped((w, slots), BF16)
    turned = shaped((slots, w), BF16)
    cross = shaped((slots, rows))
    halves = shaped(operators.shape, BF16)
    pick, weight, hit, live, column, ops_high, ops_low = run(
        prepare_kernel,
        [shaped((rows, slots), BF16), cross, cross, shaped((slots, 1)), shaped((*operator_state.shape, 1)),
         halves, halves],
        [counts], sources[0], targets[0], negatives[0], operators, operator_state, name="prepare",
    )
    x_high, x_low, unit, scale, turned_high, turned_low = run(
        left_kernel,
        [wide, wide, shaped((w, slots)), shaped((1, slots)), turned, turned],
        [], left, ops_high, ops_low, pick, rel, after=[left_sum], flops=2 * 10**9, name="left_side",
    )
    square = shaped((slots, rows), BF16)
    send, d_high, d_low, p_high, p_low = run(
        right_kernel,
        [shaped((packed, LANES)), wide, wide, square, square],
        [], right, unit, scale, turned_high, turned_low, weight, hit, live, rel, x_high, x_low,
        after=[right_sum], flops=3 * 10**9, name="right_side",
    )
    got = across_cores(send)
    keep = run(
        keep_kernel, shaped((packed, LANES)), [], rel, d_high, d_low, x_high, x_low,
        flops=10**9, name="own_relation",
    )

    part = shaped((packed // chips // 2, LANES))
    direct, distant = peers_of(chips)
    bundle = shaped((len(distant), *part.shape))
    dealt = run(
        deal_kernel, ([part] * len(direct) + [bundle]) * 2, [],
        *[t.reshape(chips, 2, *part.shape) for t in (keep, got)], name="sum_cores",
    )
    away, home = dealt[:len(direct)], dealt[len(direct) + 1:-1]
    merged = run(
        merge_kernel, [part] * len(distant), [], dealt[-1], swap(dealt[len(direct)], "rhs", 1), name="merge_layers",
    )
    away = [away[0]] + [across_chips(t, j) for j, t in zip(direct[1:], away[1:])]
    home = [home[0]] + [across_chips(t, j) for j, t in zip(direct[1:] + distant, home[1:] + merged)]
    passed = run(functools.partial(sum_kernel, after=0), part, [], *away, name="sum_away")
    done = shaped((8, LANES))
    new_left, done_left = run(
        left_update_kernel, [shaped((w, rows)), done],
        [], left, left_sum, ops_high, ops_low, pick, rel, d_high, d_low,
        after=[passed], flops=2 * 10**9, name="left_update",
    )
    mine = run(
        functools.partial(sum_kernel, after=1), part, [], *home, swap(passed, "rhs", 1),
        after=[done_left], name="sum_home",
    )
    new_right, done_right = run(
        right_update_kernel, [shaped((w, rows)), done],
        [], right, right_sum, unit, p_high, p_low,
        after=[mine], flops=10**9, name="right_update",
    )
    bit, after = 2, [done_right]
    while bit < layers:
        mine = run(
            functools.partial(sum_kernel, after=len(after)), part,
            [], mine, swap(mine, "rhs", bit), after=after, name="sum_layers",
        )
        bit, after = 2 * bit, []
    next_layer = swap(mine, "rhs", 1)

    def spread(value):
        taken = [value]
        for j in walk_of(chips)[1:]:
            taken.append(run(copy_kernel, part, [], across_chips(value, j), after=taken[-1:], name="take"))
        return taken

    joined = shaped((chips, *part.shape))
    near = run(join_kernel, joined, [], *spread(mine), name="join_near")
    far = run(join_kernel, joined, [], *spread(next_layer), name="join_far")
    other_near, other_far = across_cores(near), across_cores(far)
    flat = [pltpu.VMEM((packed, LANES), F32)]
    own = run(
        own_operator_kernel, shaped(operators.shape[1:]), [], operators, column, near, far,
        scratch=flat, name="own_operator",
    )
    new_operators = run(
        operator_kernel, shaped(operators.shape), [], own, operators, column, other_near, other_far,
        scratch=[*flat, pltpu.VMEM(operators.shape[1:], F32), pltpu.SemaphoreType.DMA((2,))],
        out_specs=ANY, name="operator_update",
    )
    return (
        jnp.swapaxes(new_left, 0, 1)[None, None],
        jnp.swapaxes(new_right, 0, 1)[None, None],
        new_operators,
    )


def solution(mesh):
    return jax.shard_map(
        body,
        mesh=mesh,
        in_specs=(
            P("lhs", "rhs", None, None),
            P("lhs", "rhs", None),
            P("lhs", "rhs", None, None),
            P("lhs", "rhs", None),
            P(),
            P(),
            P("lhs", "rhs", None),
            P("lhs", "rhs", None),
            P("lhs", "rhs", None),
            P("lhs", "rhs", None),
            P("lhs", "rhs"),
        ),
        out_specs=(P("lhs", "rhs", None, None), P("lhs", "rhs", None, None), P()),
        check_vma=False,
    )
```

```python
import functools

import jax
import jax.numpy as jnp
from jax import lax
from jax.experimental import pallas as pl
from jax.experimental.pallas import tpu as pltpu
from jax.sharding import PartitionSpec as P

F32 = jnp.float32
BF16 = jnp.bfloat16
LANES = 128
NN = ((1,), (0,))
NT = ((1,), (1,))
TN = ((0,), (0,))
EPS = 1e-06


def cut(x):
    high = x.astype(BF16)
    low = (x - high.astype(F32)).astype(BF16)
    return high, low


def mul(a, b, dims):
    return lax.dot_general(a, b, (dims, ((), ())), preferred_element_type=F32)


def mul3(a, b, dims):
    return mul(a[0], b[0], dims) + (mul(a[0], b[1], dims) + mul(a[1], b[0], dims))


def deep3(a, b, dims):
    (da,), (db,) = dims
    left = jnp.concatenate([a[0], a[0], a[1]], axis=da)
    right = jnp.concatenate([b[0], b[1], b[0]], axis=db)
    return mul(left, right, dims)


def one_hot(index_row, rows):
    shape = (rows, index_row.shape[1])
    return lax.broadcasted_iota(jnp.int32, shape, 0) == index_row


def prepare_kernel(
    count, src, tgt, neg, ops, op_sums,
    pick, weight, hit, live, column, ops_high, ops_low,
):
    rows, slots = pick.shape
    w = ops.shape[1]
    pick[...] = one_hot(src[...], rows).astype(BF16)
    target = jnp.transpose(one_hot(tgt[...], rows).astype(F32))
    sample = jnp.transpose(one_hot(neg[...], rows).astype(F32))
    alive = (lax.broadcasted_iota(jnp.int32, (slots, 1), 0) < count[0, 0]).astype(F32)
    weight[...] = target + jnp.sum(sample, axis=0, keepdims=True)
    hit[...] = target * alive
    live[...] = alive
    diagonal = one_hot(lax.broadcasted_iota(jnp.int32, (1, w), 1), w)
    for i in range(ops.shape[0]):
        column[i] = jnp.sum(jnp.where(diagonal, op_sums[i:i + 1, :], 0.0), axis=1, keepdims=True)
        high, low = cut(ops[i])
        ops_high[i] = high
        ops_low[i] = low


def left_kernel(after, left, ops_high, ops_low, pick, rel, x_high, x_low, unit, scale, turned_high, turned_low):
    high, low = cut(left[...])
    xh = mul(high, pick[...], NN).astype(BF16)
    xl = mul(low, pick[...], NN).astype(BF16)
    x_high[...] = xh
    x_low[...] = xl
    first = mul3((ops_high[0], ops_low[0]), (xh, xl), TN)
    second = mul3((ops_high[1], ops_low[1]), (xh, xl), TN)
    mapped = jnp.where(rel[...] == 0, first, second)
    inv = lax.rsqrt(jnp.sum(mapped * mapped, axis=0, keepdims=True) + EPS)
    u = mapped * inv
    unit[...] = u
    scale[...] = inv
    high, low = cut(jnp.transpose(u))
    turned_high[...] = high
    turned_low[...] = low


def operator_grad(which, relations, d_high, d_low, x, out):
    own = relations == which
    masked = [jnp.where(own, part.astype(F32), 0.0).astype(BF16) for part in (d_high, d_low)]
    grad = deep3(x, masked, NT)
    w = grad.shape[0]
    tiles, rest = w // LANES, w % LANES
    for t in range(tiles):
        out[pl.ds(t * w, w), :] = grad[:, t * LANES:(t + 1) * LANES]
    tail = jnp.transpose(grad[:, tiles * LANES:])
    base = tiles * w
    out[pl.ds(base, out.shape[0] - base), :] = jnp.zeros((out.shape[0] - base, LANES), F32)
    for t in range(-(-w // LANES)):
        width = min(LANES, w - t * LANES)
        out[pl.ds(base + t * rest, rest), 0:width] = tail[:, t * LANES:t * LANES + width]


def right_kernel(
    after, right, unit, scale, turned_high, turned_low, weight, hit, live, rel, x_high, x_low,
    send, d_high, d_low, p_high, p_low,
):
    r = right[...]
    split = cut(r)
    inv = lax.rsqrt(jnp.sum(r * r, axis=0, keepdims=True) + EPS)
    scores = mul3((turned_high[...], turned_low[...]), split, NN) * inv
    weighted = jnp.exp(scores) * weight[...]
    total = jnp.sum(weighted, axis=1, keepdims=True)
    push = weighted * (live[...] / total) - hit[...]
    p_high[...], p_low[...] = cut(push)
    du = deep3(split, cut(push * inv), NT)
    u = unit[...]
    along = jnp.sum(u * du, axis=0, keepdims=True)
    dh, dl = cut(scale[...] * (du - u * along))
    d_high[...] = dh
    d_low[...] = dl
    operator_grad(1 - core(), rel[...], dh, dl, (x_high[...], x_low[...]), send)


def keep_kernel(rel, d_high, d_low, x_high, x_low, keep):
    operator_grad(core(), rel[...], d_high[...], d_low[...], (x_high[...], x_low[...]), keep)


def adagrad_t(weights, sums, grad):
    summed = sums + jnp.sum(grad * grad, axis=0, keepdims=True) / grad.shape[0]
    return weights - grad * (0.1 / jnp.sqrt(summed))


def left_update_kernel(
    after, left, left_sum, ops_high, ops_low, pick, rel, d_high, d_low, new_left, done,
):
    d = (d_high[...], d_low[...])
    first = mul3((ops_high[0], ops_low[0]), d, NN)
    second = mul3((ops_high[1], ops_low[1]), d, NN)
    dx = cut(jnp.where(rel[...] == 0, first, second))
    grad = mul(dx[0], pick[...], NT) + mul(dx[1], pick[...], NT)
    new_left[...] = adagrad_t(left[...], left_sum[...], grad)
    done[...] = jnp.zeros_like(done)


def right_update_kernel(after, right, right_sum, unit, p_high, p_low, new_right, done):
    r = right[...]
    inv = lax.rsqrt(jnp.sum(r * r, axis=0, keepdims=True) + EPS)
    v = r * inv
    dv = deep3(cut(unit[...]), (p_high[...], p_low[...]), NN)
    grad = inv * (dv - v * jnp.sum(v * dv, axis=0, keepdims=True))
    new_right[...] = adagrad_t(r, right_sum[...], grad)
    done[...] = jnp.zeros_like(done)


def core():
    return lax.rem(lax.axis_index("lhs"), 2)


def chip():
    return lax.div(lax.axis_index("lhs"), 2)


def side():
    return lax.rem(lax.axis_index("rhs"), 2)


def deal_kernel(one, two, *outs):
    direct, distant = peers_of(one.shape[0])
    for half, own in enumerate((1 - side(), side())):
        own_outs = outs[half * (len(direct) + 1):]

        def part(j):
            spot = jnp.bitwise_xor(chip(), j)
            return one[spot, own] + two[spot, own]

        for j, out in zip(direct, own_outs):
            out[...] = part(j)
        for i, j in enumerate(distant):
            own_outs[len(direct)][i] = part(j)


def merge_kernel(one, two, *outs):
    for i, out in enumerate(outs):
        out[...] = one[i] + two[i]


def sum_kernel(*refs, after):
    refs = refs[after:]
    refs[-1][...] = functools.reduce(jnp.add, [ref[...] for ref in refs[:-1]])


def join_kernel(*refs, after=0):
    out = refs[-1]
    for j, ref in zip(walk_of(out.shape[0]), refs[after:]):
        out[jnp.bitwise_xor(chip(), j)] = ref[...]


def copy_kernel(after, value, out):
    out[...] = value[...]


def operator_rows(which, ops, sums, near, far, flat, out, finish):
    chunk = near.shape[1]
    for j in range(near.shape[0]):
        for own, ref in ((side(), near), (1 - side(), far)):
            flat[pl.ds(pl.multiple_of((2 * j + own) * chunk, 8), chunk), :] = ref[j]
    w = ops.shape[1]
    main = w // LANES
    rest = w - main * LANES
    tiles = [flat[pl.ds(t * w, w), :] for t in range(main)]
    tail = jnp.concatenate(
        [flat[pl.ds(main * w + t * rest, rest), :] for t in range(-(-w // LANES))], axis=1
    )
    tail = jnp.transpose(tail)[:w]
    square = jnp.sum(tail * tail, axis=1, keepdims=True)
    square = square + jnp.sum(sum(tile * tile for tile in tiles), axis=1, keepdims=True)
    rate = 0.1 / jnp.sqrt(sums[which] + square / w)
    for block in (slice(0, w // 16 * 8), slice(w // 16 * 8, w)):
        for t, part in enumerate([*tiles, tail]):
            span = slice(t * LANES, min(w, (t + 1) * LANES))
            out[block, span] = ops[which, block, span] - part[block] * rate[block]
        finish(block)


def own_operator_kernel(ops, sums, near, far, out, flat):
    operator_rows(core(), ops, sums, near, far, flat, out, lambda block: None)


def operator_kernel(own, ops, sums, near, far, out, flat, half, sem):
    copies = [pltpu.make_async_copy(own, out.at[core()], sem.at[0])]
    copies[0].start()

    def finish(block):
        target = out.at[1 - core(), block, :]
        copies.append(pltpu.make_async_copy(half.at[block, :], target, sem.at[len(copies)]))
        copies[-1].start()

    operator_rows(1 - core(), ops, sums, near, far, flat, half, finish)
    for copy in copies:
        copy.wait()


def shaped(shape, dtype=F32):
    return jax.ShapeDtypeStruct(shape, dtype)


VMEM = pl.BlockSpec(memory_space=pltpu.VMEM)
ANY = pl.BlockSpec(memory_space=pl.ANY)
SMEM = pl.BlockSpec(memory_space=pltpu.SMEM)


def run(kernel, out_shape, scalars, *args, after=(), scratch=(), out_specs=None, flops=0, size=2**20, name=None):
    specs = [SMEM] * len(scalars) + [ANY] * len(after) + [VMEM] * len(args)
    return pl.pallas_call(
        kernel,
        out_shape=out_shape,
        in_specs=specs,
        out_specs=out_specs or jax.tree.map(lambda _: VMEM, out_shape),
        scratch_shapes=scratch,
        compiler_params=pltpu.CompilerParams(vmem_limit_bytes=24 * 2**20),
        cost_estimate=pl.CostEstimate(flops=flops, bytes_accessed=size, transcendentals=0),
        name=name,
    )(*scalars, *after, *args)


def around(value, axis, steps):
    count = lax.axis_size(axis)
    return lax.ppermute(value, axis, [(i, (i + steps) % count) for i in range(count)])


def swap(value, axis, bit):
    count = lax.axis_size(axis)
    return lax.ppermute(value, axis, [(i, i ^ bit) for i in range(count)])


def across_cores(value):
    return swap(value, "lhs", 1)


def peers_of(count):
    return [j for j in range(count) if j.bit_count() < 2], [j for j in range(count) if j.bit_count() > 1]


def walk_of(count):
    return [j ^ (j // 2) for j in range(count)]


def across_chips(value, j):
    return swap(value, "lhs", 2 * j)


def body(
    left_table, left_state, right_table, right_state, operators, operator_state,
    sources, targets, relations, negatives, counts,
):
    rows, w = left_table.shape[2:]
    slots = sources.shape[2]
    chips = lax.axis_size("lhs") // 2
    layers = lax.axis_size("rhs")
    unit_rows = 16 * chips
    used = w // LANES * w + (w % LANES) * -(-w // LANES)
    packed = -(-used // unit_rows) * unit_rows

    right = around(jnp.swapaxes(right_table[0, 0], 0, 1), "rhs", 1)
    left = around(jnp.swapaxes(left_table[0, 0], 0, 1), "lhs", 1)
    left_sum = around(left_state[0], "lhs", 1)
    right_sum = around(right_state[0], "rhs", 1)
    rel = relations[0]
    wide = shaped((w, slots), BF16)
    turned = shaped((slots, w), BF16)
    cross = shaped((slots, rows))
    halves = shaped(operators.shape, BF16)
    pick, weight, hit, live, column, ops_high, ops_low = run(
        prepare_kernel,
        [shaped((rows, slots), BF16), cross, cross, shaped((slots, 1)), shaped((*operator_state.shape, 1)),
         halves, halves],
        [counts], sources[0], targets[0], negatives[0], operators, operator_state, name="prepare",
    )
    x_high, x_low, unit, scale, turned_high, turned_low = run(
        left_kernel,
        [wide, wide, shaped((w, slots)), shaped((1, slots)), turned, turned],
        [], left, ops_high, ops_low, pick, rel, after=[left_sum], flops=2 * 10**9, name="left_side",
    )
    square = shaped((slots, rows), BF16)
    send, d_high, d_low, p_high, p_low = run(
        right_kernel,
        [shaped((packed, LANES)), wide, wide, square, square],
        [], right, unit, scale, turned_high, turned_low, weight, hit, live, rel, x_high, x_low,
        after=[right_sum], flops=3 * 10**9, name="right_side",
    )
    got = across_cores(send)
    keep = run(
        keep_kernel, shaped((packed, LANES)), [], rel, d_high, d_low, x_high, x_low,
        flops=10**9, name="own_relation",
    )

    part = shaped((packed // chips // 2, LANES))
    direct, distant = peers_of(chips)
    bundle = shaped((len(distant), *part.shape))
    dealt = run(
        deal_kernel, ([part] * len(direct) + [bundle]) * 2, [],
        *[t.reshape(chips, 2, *part.shape) for t in (keep, got)], name="sum_cores",
    )
    away, home = dealt[:len(direct)], dealt[len(direct) + 1:-1]
    merged = run(
        merge_kernel, [part] * len(distant), [], dealt[-1], swap(dealt[len(direct)], "rhs", 1), name="merge_layers",
    )
    away = [away[0]] + [across_chips(t, j) for j, t in zip(direct[1:], away[1:])]
    home = [home[0]] + [across_chips(t, j) for j, t in zip(direct[1:] + distant, home[1:] + merged)]
    passed = run(functools.partial(sum_kernel, after=1), part, [], *away, after=merged[:1], name="sum_away")
    done = shaped((8, LANES))
    mine = run(
        functools.partial(sum_kernel, after=0), part, [], *home, swap(passed, "rhs", 1), name="sum_home",
    )
    new_left, done_left = run(
        left_update_kernel, [shaped((w, rows)), done],
        [], left, left_sum, ops_high, ops_low, pick, rel, d_high, d_low,
        after=[mine], flops=2 * 10**9, name="left_update",
    )
    bit, after = 2, [done_left]
    while bit < layers:
        mine = run(
            functools.partial(sum_kernel, after=len(after)), part,
            [], mine, swap(mine, "rhs", bit), after=after, name="sum_layers",
        )
        bit, after = 2 * bit, []
    next_layer = swap(mine, "rhs", 1)

    def spread(value):
        taken = [value]
        for j in walk_of(chips)[1:]:
            taken.append(run(copy_kernel, part, [], across_chips(value, j), after=taken[-1:], name="take"))
        return taken

    joined = shaped((chips, *part.shape))
    near = run(join_kernel, joined, [], *spread(mine), name="join_near")
    new_right, done_right = run(
        right_update_kernel, [shaped((w, rows)), done],
        [], right, right_sum, unit, p_high, p_low,
        after=[near], size=0, name="right_update",
    )
    far = run(
        functools.partial(join_kernel, after=1), joined, [], *spread(next_layer), after=[done_right], name="join_far",
    )
    other_near, other_far = across_cores(near), across_cores(far)
    flat = [pltpu.VMEM((packed, LANES), F32)]
    own = run(
        own_operator_kernel, shaped(operators.shape[1:]), [], operators, column, near, far,
        scratch=flat, name="own_operator",
    )
    new_operators = run(
        operator_kernel, shaped(operators.shape), [], own, operators, column, other_near, other_far,
        scratch=[*flat, pltpu.VMEM(operators.shape[1:], F32), pltpu.SemaphoreType.DMA((3,))],
        out_specs=ANY, name="operator_update",
    )
    return (
        jnp.swapaxes(new_left, 0, 1)[None, None],
        jnp.swapaxes(new_right, 0, 1)[None, None],
        new_operators,
    )


def solution(mesh):
    return jax.shard_map(
        body,
        mesh=mesh,
        in_specs=(
            P("lhs", "rhs", None, None),
            P("lhs", "rhs", None),
            P("lhs", "rhs", None, None),
            P("lhs", "rhs", None),
            P(),
            P(),
            P("lhs", "rhs", None),
            P("lhs", "rhs", None),
            P("lhs", "rhs", None),
            P("lhs", "rhs", None),
            P("lhs", "rhs"),
        ),
        out_specs=(P("lhs", "rhs", None, None), P("lhs", "rhs", None, None), P()),
        check_vma=False,
    )
```

```python
import functools

import jax
import jax.numpy as jnp
from jax import lax
from jax.experimental import pallas as pl
from jax.experimental.pallas import tpu as pltpu
from jax.sharding import PartitionSpec as P

F32 = jnp.float32
BF16 = jnp.bfloat16
LANES = 128
NN = ((1,), (0,))
NT = ((1,), (1,))
TN = ((0,), (0,))
EPS = 1e-06


def cut(x):
    high = x.astype(BF16)
    low = (x - high.astype(F32)).astype(BF16)
    return high, low


def mul(a, b, dims):
    return lax.dot_general(a, b, (dims, ((), ())), preferred_element_type=F32)


def mul3(a, b, dims):
    return mul(a[0], b[0], dims) + (mul(a[0], b[1], dims) + mul(a[1], b[0], dims))


def deep3(a, b, dims):
    (da,), (db,) = dims
    left = jnp.concatenate([a[0], a[0], a[1]], axis=da)
    right = jnp.concatenate([b[0], b[1], b[0]], axis=db)
    return mul(left, right, dims)


def one_hot(index_row, rows):
    shape = (rows, index_row.shape[1])
    return lax.broadcasted_iota(jnp.int32, shape, 0) == index_row


def prepare_kernel(
    count, src, tgt, neg, ops, op_sums,
    pick, weight, hit, live, column, ops_high, ops_low,
):
    rows, slots = pick.shape
    w = ops.shape[1]
    pick[...] = one_hot(src[...], rows).astype(BF16)
    target = jnp.transpose(one_hot(tgt[...], rows).astype(F32))
    sample = jnp.transpose(one_hot(neg[...], rows).astype(F32))
    alive = (lax.broadcasted_iota(jnp.int32, (slots, 1), 0) < count[0, 0]).astype(F32)
    weight[...] = target + jnp.sum(sample, axis=0, keepdims=True)
    hit[...] = target * alive
    live[...] = alive
    diagonal = one_hot(lax.broadcasted_iota(jnp.int32, (1, w), 1), w)
    for i in range(ops.shape[0]):
        column[i] = jnp.sum(jnp.where(diagonal, op_sums[i:i + 1, :], 0.0), axis=1, keepdims=True)
        high, low = cut(ops[i])
        ops_high[i] = high
        ops_low[i] = low


def left_kernel(after, left, ops_high, ops_low, pick, rel, x_high, x_low, unit, scale, turned):
    high, low = cut(left[...])
    xh = mul(high, pick[...], NN).astype(BF16)
    xl = mul(low, pick[...], NN).astype(BF16)
    x_high[...] = xh
    x_low[...] = xl
    first = mul3((ops_high[0], ops_low[0]), (xh, xl), TN)
    second = mul3((ops_high[1], ops_low[1]), (xh, xl), TN)
    mapped = jnp.where(rel[...] == 0, first, second)
    inv = lax.rsqrt(jnp.sum(mapped * mapped, axis=0, keepdims=True) + EPS)
    u = mapped * inv
    unit[...] = u
    scale[...] = inv
    high, low = cut(jnp.transpose(u))
    turned[...] = jnp.concatenate([high, high, low], axis=1)


def operator_grad(which, relations, d_high, d_low, x, out):
    own = relations == which
    masked = [jnp.where(own, part.astype(F32), 0.0).astype(BF16) for part in (d_high, d_low)]
    grad = deep3(x, masked, NT)
    w = grad.shape[0]
    tiles, rest = w // LANES, w % LANES
    for t in range(tiles):
        out[pl.ds(t * w, w), :] = grad[:, t * LANES:(t + 1) * LANES]
    tail = jnp.transpose(grad[:, tiles * LANES:])
    base = tiles * w
    out[pl.ds(base, out.shape[0] - base), :] = jnp.zeros((out.shape[0] - base, LANES), F32)
    for t in range(-(-w // LANES)):
        width = min(LANES, w - t * LANES)
        out[pl.ds(base + t * rest, rest), 0:width] = tail[:, t * LANES:t * LANES + width]


def right_kernel(
    after, right, unit, scale, turned, weight, hit, live, rel, x_high, x_low,
    send, d_high, d_low, p_high, p_low,
):
    r = right[...]
    split = cut(r)
    inv = lax.rsqrt(jnp.sum(r * r, axis=0, keepdims=True) + EPS)
    scores = mul(turned[...], jnp.concatenate([split[0], split[1], split[0]], axis=0), NN) * inv
    weighted = jnp.exp(scores) * weight[...]
    total = jnp.sum(weighted, axis=1, keepdims=True)
    push = weighted * (live[...] / total) - hit[...]
    p_high[...], p_low[...] = cut(push)
    du = deep3(split, cut(push * inv), NT)
    u = unit[...]
    along = jnp.sum(u * du, axis=0, keepdims=True)
    dh, dl = cut(scale[...] * (du - u * along))
    d_high[...] = dh
    d_low[...] = dl
    operator_grad(1 - core(), rel[...], dh, dl, (x_high[...], x_low[...]), send)


def keep_kernel(rel, d_high, d_low, x_high, x_low, keep):
    operator_grad(core(), rel[...], d_high[...], d_low[...], (x_high[...], x_low[...]), keep)


def adagrad_t(weights, sums, grad):
    summed = sums + jnp.sum(grad * grad, axis=0, keepdims=True) / grad.shape[0]
    return weights - grad * (0.1 / jnp.sqrt(summed))


def left_update_kernel(
    after, left, left_sum, ops_high, ops_low, pick, rel, d_high, d_low, new_left, done,
):
    d = (d_high[...], d_low[...])
    first = mul3((ops_high[0], ops_low[0]), d, NN)
    second = mul3((ops_high[1], ops_low[1]), d, NN)
    dx = cut(jnp.where(rel[...] == 0, first, second))
    grad = mul(dx[0], pick[...], NT) + mul(dx[1], pick[...], NT)
    new_left[...] = adagrad_t(left[...], left_sum[...], grad)
    done[...] = jnp.zeros_like(done)


def right_update_kernel(after, right, right_sum, unit, p_high, p_low, new_right, done):
    r = right[...]
    inv = lax.rsqrt(jnp.sum(r * r, axis=0, keepdims=True) + EPS)
    v = r * inv
    dv = deep3(cut(unit[...]), (p_high[...], p_low[...]), NN)
    grad = inv * (dv - v * jnp.sum(v * dv, axis=0, keepdims=True))
    new_right[...] = adagrad_t(r, right_sum[...], grad)
    done[...] = jnp.zeros_like(done)


def core():
    return lax.rem(lax.axis_index("lhs"), 2)


def chip():
    return lax.div(lax.axis_index("lhs"), 2)


def side():
    return lax.rem(lax.axis_index("rhs"), 2)


def deal_kernel(one, two, *outs):
    direct, distant = peers_of(one.shape[0])
    for half, own in enumerate((1 - side(), side())):
        own_outs = outs[half * (len(direct) + 1):]

        def part(j):
            spot = jnp.bitwise_xor(chip(), j)
            return one[spot, own] + two[spot, own]

        for j, out in zip(direct, own_outs):
            out[...] = part(j)
        for i, j in enumerate(distant):
            own_outs[len(direct)][i] = part(j)


def merge_kernel(one, two, *outs):
    for i, out in enumerate(outs):
        out[...] = one[i] + two[i]


def sum_kernel(*refs, after):
    refs = refs[after:]
    refs[-1][...] = functools.reduce(jnp.add, [ref[...] for ref in refs[:-1]])


def join_kernel(*refs, after=0):
    out = refs[-1]
    direct, distant = peers_of(out.shape[0])
    rest = refs[after + len(direct):-1]
    for j, ref in zip(direct, refs[after:]):
        out[jnp.bitwise_xor(chip(), j)] = ref[...]
    for i, j in enumerate(distant):
        out[jnp.bitwise_xor(chip(), j)] = rest[0][i] if len(rest[0].shape) == 3 else rest[i][...]


def stack_kernel(*refs):
    for i, ref in enumerate(refs[:-1]):
        refs[-1][i] = ref[...]


def operator_rows(which, ops, sums, near, far, flat, out, finish):
    chunk = near.shape[1]
    for j in range(near.shape[0]):
        for own, ref in ((side(), near), (1 - side(), far)):
            flat[pl.ds(pl.multiple_of((2 * j + own) * chunk, 8), chunk), :] = ref[j]
    w = ops.shape[1]
    main = w // LANES
    rest = w - main * LANES
    tiles = [flat[pl.ds(t * w, w), :] for t in range(main)]
    tail = jnp.concatenate(
        [flat[pl.ds(main * w + t * rest, rest), :] for t in range(-(-w // LANES))], axis=1
    )
    tail = jnp.transpose(tail)[:w]
    square = jnp.sum(tail * tail, axis=1, keepdims=True)
    square = square + jnp.sum(sum(tile * tile for tile in tiles), axis=1, keepdims=True)
    rate = 0.1 / jnp.sqrt(sums[which] + square / w)
    for block in (slice(0, w // 16 * 8), slice(w // 16 * 8, w)):
        for t, part in enumerate([*tiles, tail]):
            span = slice(t * LANES, min(w, (t + 1) * LANES))
            out[block, span] = ops[which, block, span] - part[block] * rate[block]
        finish(block)


def operator_kernel(ops, sums, near, far, *refs, own):
    out, flat, half, sem = refs[-4:]
    which = core() if own else 1 - core()
    copies = []

    def finish(block):
        target = out.at[which, block, :]
        copies.append(pltpu.make_async_copy(half.at[block, :], target, sem.at[len(copies)]))
        copies[-1].start()

    operator_rows(which, ops, sums, near, far, flat, half, finish)
    for copy in copies:
        copy.wait()


def shaped(shape, dtype=F32):
    return jax.ShapeDtypeStruct(shape, dtype)


VMEM = pl.BlockSpec(memory_space=pltpu.VMEM)
ANY = pl.BlockSpec(memory_space=pl.ANY)
HBM = pl.BlockSpec(memory_space=pltpu.HBM)
SMEM = pl.BlockSpec(memory_space=pltpu.SMEM)


def run(kernel, out_shape, scalars, *args, after=(), scratch=(), out_specs=None, in_place=False, flops=0, size=2**20, name=None):
    specs = [SMEM] * len(scalars) + [ANY] * len(after) + [VMEM] * len(args)
    if in_place:
        specs[-1] = HBM
    return pl.pallas_call(
        kernel,
        out_shape=out_shape,
        in_specs=specs,
        out_specs=out_specs or jax.tree.map(lambda _: VMEM, out_shape),
        scratch_shapes=scratch,
        input_output_aliases={len(specs) - 1: 0} if in_place else {},
        compiler_params=pltpu.CompilerParams(vmem_limit_bytes=24 * 2**20),
        cost_estimate=pl.CostEstimate(flops=flops, bytes_accessed=size, transcendentals=0),
        name=name,
    )(*scalars, *after, *args)


def around(value, axis, steps):
    count = lax.axis_size(axis)
    return lax.ppermute(value, axis, [(i, (i + steps) % count) for i in range(count)])


def swap(value, axis, bit):
    count = lax.axis_size(axis)
    return lax.ppermute(value, axis, [(i, i ^ bit) for i in range(count)])


def across_cores(value):
    return swap(value, "lhs", 1)


def peers_of(count):
    return [j for j in range(count) if j.bit_count() < 2], [j for j in range(count) if j.bit_count() > 1]


def across_chips(value, j):
    return swap(value, "lhs", 2 * j)


def body(
    left_table, left_state, right_table, right_state, operators, operator_state,
    sources, targets, relations, negatives, counts,
):
    rows, w = left_table.shape[2:]
    slots = sources.shape[2]
    chips = lax.axis_size("lhs") // 2
    layers = lax.axis_size("rhs")
    unit_rows = 16 * chips
    used = w // LANES * w + (w % LANES) * -(-w // LANES)
    packed = -(-used // unit_rows) * unit_rows

    right = around(jnp.swapaxes(right_table[0, 0], 0, 1), "rhs", 1)
    left = around(jnp.swapaxes(left_table[0, 0], 0, 1), "lhs", 1)
    left_sum = around(left_state[0], "lhs", 1)
    right_sum = around(right_state[0], "rhs", 1)
    rel = relations[0]
    wide = shaped((w, slots), BF16)
    turned = shaped((slots, 3 * w), BF16)
    cross = shaped((slots, rows))
    halves = shaped(operators.shape, BF16)
    pick, weight, hit, live, column, ops_high, ops_low = run(
        prepare_kernel,
        [shaped((rows, slots), BF16), cross, cross, shaped((slots, 1)), shaped((*operator_state.shape, 1)),
         halves, halves],
        [counts], sources[0], targets[0], negatives[0], operators, operator_state, name="prepare",
    )
    x_high, x_low, unit, scale, turned = run(
        left_kernel,
        [wide, wide, shaped((w, slots)), shaped((1, slots)), turned],
        [], left, ops_high, ops_low, pick, rel, after=[left_sum], flops=2 * 10**9, name="left_side",
    )
    square = shaped((slots, rows), BF16)
    send, d_high, d_low, p_high, p_low = run(
        right_kernel,
        [shaped((packed, LANES)), wide, wide, square, square],
        [], right, unit, scale, turned, weight, hit, live, rel, x_high, x_low,
        after=[right_sum], flops=3 * 10**9, name="right_side",
    )
    got = across_cores(send)
    keep = run(
        keep_kernel, shaped((packed, LANES)), [], rel, d_high, d_low, x_high, x_low,
        flops=10**9, name="own_relation",
    )

    part = shaped((packed // chips // 2, LANES))
    direct, distant = peers_of(chips)
    bundle = shaped((len(distant), *part.shape))
    dealt = run(
        deal_kernel, ([part] * len(direct) + [bundle]) * 2, [],
        *[t.reshape(chips, 2, *part.shape) for t in (keep, got)], name="sum_cores",
    )
    away, home = dealt[:len(direct)], dealt[len(direct) + 1:-1]
    merged = run(
        merge_kernel, [part] * len(distant), [], dealt[-1], swap(dealt[len(direct)], "rhs", 1), name="merge_layers",
    )
    away = [away[0]] + [across_chips(t, j) for j, t in zip(direct[1:], away[1:])]
    home = [home[0]] + [across_chips(t, j) for j, t in zip(direct[1:] + distant, home[1:] + merged)]
    passed = run(functools.partial(sum_kernel, after=1), part, [], *away, after=merged[:1], name="sum_away")
    done = shaped((8, LANES))
    mine = run(
        functools.partial(sum_kernel, after=0), part, [], *home, swap(passed, "rhs", 1), name="sum_home",
    )
    new_left, done_left = run(
        left_update_kernel, [shaped((w, rows)), done],
        [], left, left_sum, ops_high, ops_low, pick, rel, d_high, d_low,
        after=[mine], flops=2 * 10**9, name="left_update",
    )
    bit, after = 2, [done_left]
    while bit < layers:
        mine = run(
            functools.partial(sum_kernel, after=len(after)), part,
            [], mine, swap(mine, "rhs", bit), after=after, name="sum_layers",
        )
        bit, after = 2 * bit, []
    next_layer = swap(mine, "rhs", 1)

    distant_parts = [across_chips(mine, j) for j in distant]
    if len(distant) > 1:
        handed = [swap(run(stack_kernel, bundle, [], *distant_parts, name="stack_distant"), "rhs", 1)]
    else:
        handed = [swap(t, "rhs", 1) for t in distant_parts]

    def spread(value):
        return [value] + [across_chips(value, j) for j in direct[1:]]

    joined = shaped((chips, *part.shape))
    near = run(join_kernel, joined, [], *spread(mine), *distant_parts, name="join_near")
    new_right, done_right = run(
        right_update_kernel, [shaped((w, rows)), done],
        [], right, right_sum, unit, p_high, p_low,
        after=[near], size=0, name="right_update",
    )
    far = run(
        functools.partial(join_kernel, after=1), joined, [], *spread(next_layer), *handed, after=[done_right], name="join_far",
    )
    other_near, other_far = across_cores(near), across_cores(far)
    scratch = [
        pltpu.VMEM((packed, LANES), F32), pltpu.VMEM(operators.shape[1:], F32), pltpu.SemaphoreType.DMA((2,)),
    ]
    half_done = run(
        functools.partial(operator_kernel, own=True), shaped(operators.shape), [], operators, column, near, far,
        scratch=scratch, out_specs=HBM, name="own_operator",
    )
    new_operators = run(
        functools.partial(operator_kernel, own=False), shaped(operators.shape),
        [], operators, column, other_near, other_far, half_done,
        scratch=scratch, out_specs=HBM, in_place=True, name="operator_update",
    )
    return (
        jnp.swapaxes(new_left, 0, 1)[None, None],
        jnp.swapaxes(new_right, 0, 1)[None, None],
        new_operators,
    )


def solution(mesh):
    return jax.shard_map(
        body,
        mesh=mesh,
        in_specs=(
            P("lhs", "rhs", None, None),
            P("lhs", "rhs", None),
            P("lhs", "rhs", None, None),
            P("lhs", "rhs", None),
            P(),
            P(),
            P("lhs", "rhs", None),
            P("lhs", "rhs", None),
            P("lhs", "rhs", None),
            P("lhs", "rhs", None),
            P("lhs", "rhs"),
        ),
        out_specs=(P("lhs", "rhs", None, None), P("lhs", "rhs", None, None), P()),
        check_vma=False,
    )
```

```python
import functools

import jax
import jax.numpy as jnp
from jax import lax
from jax.experimental import pallas as pl
from jax.experimental.pallas import tpu as pltpu
from jax.sharding import PartitionSpec as P

F32 = jnp.float32
BF16 = jnp.bfloat16
LANES = 128
NN = ((1,), (0,))
NT = ((1,), (1,))
TN = ((0,), (0,))
EPS = 1e-06


def cut(x):
    high = x.astype(BF16)
    low = (x - high.astype(F32)).astype(BF16)
    return high, low


def mul(a, b, dims):
    return lax.dot_general(a, b, (dims, ((), ())), preferred_element_type=F32)


def mul3(a, b, dims):
    return mul(a[0], b[0], dims) + (mul(a[0], b[1], dims) + mul(a[1], b[0], dims))


def deep3(a, b, dims):
    (da,), (db,) = dims
    left = jnp.concatenate([a[0], a[0], a[1]], axis=da)
    right = jnp.concatenate([b[0], b[1], b[0]], axis=db)
    return mul(left, right, dims)


def one_hot(index_row, rows):
    shape = (rows, index_row.shape[1])
    return lax.broadcasted_iota(jnp.int32, shape, 0) == index_row


def prepare_kernel(
    count, src, tgt, neg, ops, op_sums,
    pick, weight, hit, live, column, ops_high, ops_low,
):
    rows, slots = pick.shape
    w = ops.shape[1]
    pick[...] = one_hot(src[...], rows).astype(BF16)
    target = jnp.transpose(one_hot(tgt[...], rows).astype(F32))
    sample = jnp.transpose(one_hot(neg[...], rows).astype(F32))
    alive = (lax.broadcasted_iota(jnp.int32, (slots, 1), 0) < count[0, 0]).astype(F32)
    weight[...] = target + jnp.sum(sample, axis=0, keepdims=True)
    hit[...] = target * alive
    live[...] = alive
    diagonal = one_hot(lax.broadcasted_iota(jnp.int32, (1, w), 1), w)
    for i in range(ops.shape[0]):
        column[i] = jnp.sum(jnp.where(diagonal, op_sums[i:i + 1, :], 0.0), axis=1, keepdims=True)
        high, low = cut(ops[i])
        ops_high[i] = high
        ops_low[i] = low


def left_kernel(after, left, ops_high, ops_low, pick, rel, x_high, x_low, unit, scale, turned):
    high, low = cut(left[...])
    xh = mul(high, pick[...], NN).astype(BF16)
    xl = mul(low, pick[...], NN).astype(BF16)
    x_high[...] = xh
    x_low[...] = xl
    first = mul3((ops_high[0], ops_low[0]), (xh, xl), TN)
    second = mul3((ops_high[1], ops_low[1]), (xh, xl), TN)
    mapped = jnp.where(rel[...] == 0, first, second)
    inv = lax.rsqrt(jnp.sum(mapped * mapped, axis=0, keepdims=True) + EPS)
    u = mapped * inv
    unit[...] = u
    scale[...] = inv
    high, low = cut(jnp.transpose(u))
    turned[...] = jnp.concatenate([high, high, low], axis=1)


def operator_grad(which, relations, d_high, d_low, x, out):
    own = relations == which
    masked = [jnp.where(own, part.astype(F32), 0.0).astype(BF16) for part in (d_high, d_low)]
    grad = deep3(x, masked, NT)
    w = grad.shape[0]
    tiles, rest = w // LANES, w % LANES
    for t in range(tiles):
        out[pl.ds(t * w, w), :] = grad[:, t * LANES:(t + 1) * LANES]
    tail = jnp.transpose(grad[:, tiles * LANES:])
    base = tiles * w
    out[pl.ds(base, out.shape[0] - base), :] = jnp.zeros((out.shape[0] - base, LANES), F32)
    for t in range(-(-w // LANES)):
        width = min(LANES, w - t * LANES)
        out[pl.ds(base + t * rest, rest), 0:width] = tail[:, t * LANES:t * LANES + width]


def right_kernel(
    after, right, unit, scale, turned, weight, hit, live, rel, x_high, x_low,
    send, d_high, d_low, p_high, p_low,
):
    r = right[...]
    split = cut(r)
    inv = lax.rsqrt(jnp.sum(r * r, axis=0, keepdims=True) + EPS)
    scores = mul(turned[...], jnp.concatenate([split[0], split[1], split[0]], axis=0), NN) * inv
    weighted = jnp.exp(scores) * weight[...]
    total = jnp.sum(weighted, axis=1, keepdims=True)
    push = weighted * (live[...] / total) - hit[...]
    p_high[...], p_low[...] = cut(push)
    du = deep3(split, cut(push * inv), NT)
    u = unit[...]
    along = jnp.sum(u * du, axis=0, keepdims=True)
    dh, dl = cut(scale[...] * (du - u * along))
    d_high[...] = dh
    d_low[...] = dl
    operator_grad(1 - core(), rel[...], dh, dl, (x_high[...], x_low[...]), send)


def keep_kernel(rel, d_high, d_low, x_high, x_low, keep):
    operator_grad(core(), rel[...], d_high[...], d_low[...], (x_high[...], x_low[...]), keep)


def adagrad_t(weights, sums, grad):
    summed = sums + jnp.sum(grad * grad, axis=0, keepdims=True) / grad.shape[0]
    return weights - grad * (0.1 / jnp.sqrt(summed))


def left_update_kernel(
    after, left, left_sum, ops_high, ops_low, pick, rel, d_high, d_low, new_left, done,
):
    d = (d_high[...], d_low[...])
    first = mul3((ops_high[0], ops_low[0]), d, NN)
    second = mul3((ops_high[1], ops_low[1]), d, NN)
    dx = cut(jnp.where(rel[...] == 0, first, second))
    grad = mul(dx[0], pick[...], NT) + mul(dx[1], pick[...], NT)
    new_left[...] = adagrad_t(left[...], left_sum[...], grad)
    done[...] = jnp.zeros_like(done)


def right_update_kernel(after, right, right_sum, unit, p_high, p_low, new_right, done):
    r = right[...]
    inv = lax.rsqrt(jnp.sum(r * r, axis=0, keepdims=True) + EPS)
    v = r * inv
    dv = deep3(cut(unit[...]), (p_high[...], p_low[...]), NN)
    grad = inv * (dv - v * jnp.sum(v * dv, axis=0, keepdims=True))
    new_right[...] = adagrad_t(r, right_sum[...], grad)
    done[...] = jnp.zeros_like(done)


def core():
    return lax.rem(lax.axis_index("lhs"), 2)


def chip():
    return lax.div(lax.axis_index("lhs"), 2)


def side():
    return lax.rem(lax.axis_index("rhs"), 2)


def by_core(direct):
    first = core() == 0
    return [0] + [jnp.where(first, a, b) for a, b in zip(direct[1:], direct[:0:-1])]


def deal_kernel(one, two, *outs):
    direct, distant = peers_of(one.shape[0])
    for half, own in enumerate((1 - side(), side())):
        own_outs = outs[half * (len(direct) + 1):]

        def part(j):
            spot = jnp.bitwise_xor(chip(), j)
            return one[spot, own] + two[spot, own]

        for j, out in zip(by_core(direct), own_outs):
            out[...] = part(j)
        for i, j in enumerate(distant):
            own_outs[len(direct)][i] = part(j)


def merge_kernel(one, two, *outs):
    for i, out in enumerate(outs):
        out[...] = one[i] + two[i]


def sum_kernel(*refs, after):
    refs = refs[after:]
    refs[-1][...] = functools.reduce(jnp.add, [ref[...] for ref in refs[:-1]])


def join_kernel(*refs, after=0):
    out = refs[-1]
    direct, distant = peers_of(out.shape[0])
    rest = refs[after + len(direct):-1]
    for j, ref in zip(by_core(direct), refs[after:]):
        out[jnp.bitwise_xor(chip(), j)] = ref[...]
    for i, j in enumerate(distant):
        out[jnp.bitwise_xor(chip(), j)] = rest[0][i] if len(rest[0].shape) == 3 else rest[i][...]


def stack_kernel(*refs):
    for i, ref in enumerate(refs[:-1]):
        refs[-1][i] = ref[...]


def operator_rows(which, ops, sums, near, far, flat, out, finish):
    chunk = near.shape[1]
    for j in range(near.shape[0]):
        for own, ref in ((side(), near), (1 - side(), far)):
            flat[pl.ds(pl.multiple_of((2 * j + own) * chunk, 8), chunk), :] = ref[j]
    w = ops.shape[1]
    main = w // LANES
    rest = w - main * LANES
    tiles = [flat[pl.ds(t * w, w), :] for t in range(main)]
    tail = jnp.concatenate(
        [flat[pl.ds(main * w + t * rest, rest), :] for t in range(-(-w // LANES))], axis=1
    )
    tail = jnp.transpose(tail)[:w]
    square = jnp.sum(tail * tail, axis=1, keepdims=True)
    square = square + jnp.sum(sum(tile * tile for tile in tiles), axis=1, keepdims=True)
    rate = 0.1 / jnp.sqrt(sums[which] + square / w)
    for block in (slice(0, w // 16 * 8), slice(w // 16 * 8, w)):
        for t, part in enumerate([*tiles, tail]):
            span = slice(t * LANES, min(w, (t + 1) * LANES))
            out[block, span] = ops[which, block, span] - part[block] * rate[block]
        finish(block)


def operator_kernel(ops, sums, near, far, *refs, own):
    out, flat, half, sem = refs[-4:]
    which = core() if own else 1 - core()
    copies = []

    def finish(block):
        target = out.at[which, block, :]
        copies.append(pltpu.make_async_copy(half.at[block, :], target, sem.at[len(copies)]))
        copies[-1].start()

    operator_rows(which, ops, sums, near, far, flat, half, finish)
    for copy in copies:
        copy.wait()


def shaped(shape, dtype=F32):
    return jax.ShapeDtypeStruct(shape, dtype)


VMEM = pl.BlockSpec(memory_space=pltpu.VMEM)
ANY = pl.BlockSpec(memory_space=pl.ANY)
HBM = pl.BlockSpec(memory_space=pltpu.HBM)
SMEM = pl.BlockSpec(memory_space=pltpu.SMEM)


def run(kernel, out_shape, scalars, *args, after=(), scratch=(), out_specs=None, in_place=False, flops=0, size=2**20, name=None):
    specs = [SMEM] * len(scalars) + [ANY] * len(after) + [VMEM] * len(args)
    if in_place:
        specs[-1] = HBM
    return pl.pallas_call(
        kernel,
        out_shape=out_shape,
        in_specs=specs,
        out_specs=out_specs or jax.tree.map(lambda _: VMEM, out_shape),
        scratch_shapes=scratch,
        input_output_aliases={len(specs) - 1: 0} if in_place else {},
        compiler_params=pltpu.CompilerParams(vmem_limit_bytes=24 * 2**20),
        cost_estimate=pl.CostEstimate(flops=flops, bytes_accessed=size, transcendentals=0),
        name=name,
    )(*scalars, *after, *args)


def around(value, axis, steps):
    count = lax.axis_size(axis)
    return lax.ppermute(value, axis, [(i, (i + steps) % count) for i in range(count)])


def swap(value, axis, bit):
    count = lax.axis_size(axis)
    return lax.ppermute(value, axis, [(i, i ^ bit) for i in range(count)])


def across_cores(value):
    return swap(value, "lhs", 1)


def peers_of(count):
    return [j for j in range(count) if j.bit_count() < 2], [j for j in range(count) if j.bit_count() > 1]


def across_chips(value, j):
    return swap(value, "lhs", 2 * j)


def across_direct(value, spot):
    count = lax.axis_size("lhs")
    direct = peers_of(count // 2)[0]
    return lax.ppermute(value, "lhs", [(i, i ^ (2 * direct[spot if i % 2 == 0 else -spot])) for i in range(count)])


def body(
    left_table, left_state, right_table, right_state, operators, operator_state,
    sources, targets, relations, negatives, counts,
):
    rows, w = left_table.shape[2:]
    slots = sources.shape[2]
    chips = lax.axis_size("lhs") // 2
    layers = lax.axis_size("rhs")
    unit_rows = 16 * chips
    used = w // LANES * w + (w % LANES) * -(-w // LANES)
    packed = -(-used // unit_rows) * unit_rows

    right = around(jnp.swapaxes(right_table[0, 0], 0, 1), "rhs", 1)
    left = around(jnp.swapaxes(left_table[0, 0], 0, 1), "lhs", 1)
    left_sum = around(left_state[0], "lhs", 1)
    right_sum = around(right_state[0], "rhs", 1)
    rel = relations[0]
    wide = shaped((w, slots), BF16)
    turned = shaped((slots, 3 * w), BF16)
    cross = shaped((slots, rows))
    halves = shaped(operators.shape, BF16)
    pick, weight, hit, live, column, ops_high, ops_low = run(
        prepare_kernel,
        [shaped((rows, slots), BF16), cross, cross, shaped((slots, 1)), shaped((*operator_state.shape, 1)),
         halves, halves],
        [counts], sources[0], targets[0], negatives[0], operators, operator_state, name="prepare",
    )
    x_high, x_low, unit, scale, turned = run(
        left_kernel,
        [wide, wide, shaped((w, slots)), shaped((1, slots)), turned],
        [], left, ops_high, ops_low, pick, rel, after=[left_sum], flops=2 * 10**9, name="left_side",
    )
    square = shaped((slots, rows), BF16)
    send, d_high, d_low, p_high, p_low = run(
        right_kernel,
        [shaped((packed, LANES)), wide, wide, square, square],
        [], right, unit, scale, turned, weight, hit, live, rel, x_high, x_low,
        after=[right_sum], flops=3 * 10**9, name="right_side",
    )
    got = across_cores(send)
    keep = run(
        keep_kernel, shaped((packed, LANES)), [], rel, d_high, d_low, x_high, x_low,
        flops=10**9, name="own_relation",
    )

    part = shaped((packed // chips // 2, LANES))
    direct, distant = peers_of(chips)
    bundle = shaped((len(distant), *part.shape))
    dealt = run(
        deal_kernel, ([part] * len(direct) + [bundle]) * 2, [],
        *[t.reshape(chips, 2, *part.shape) for t in (keep, got)], name="sum_cores",
    )
    away, home = dealt[:len(direct)], dealt[len(direct) + 1:-1]
    merged = run(
        merge_kernel, [part] * len(distant), [], dealt[-1], swap(dealt[len(direct)], "rhs", 1), name="merge_layers",
    )
    away = [away[0]] + [across_direct(t, i + 1) for i, t in enumerate(away[1:])]
    home = [home[0]] + [across_direct(t, i + 1) for i, t in enumerate(home[1:])]
    home += [across_chips(t, j) for j, t in zip(distant, merged)]
    passed = run(functools.partial(sum_kernel, after=1), part, [], *away, after=merged[:1], name="sum_away")
    done = shaped((8, LANES))
    mine = run(
        functools.partial(sum_kernel, after=0), part, [], *home, swap(passed, "rhs", 1), name="sum_home",
    )
    new_left, done_left = run(
        left_update_kernel, [shaped((w, rows)), done],
        [], left, left_sum, ops_high, ops_low, pick, rel, d_high, d_low,
        after=[mine], flops=2 * 10**9, name="left_update",
    )
    bit, after = 2, [done_left]
    while bit < layers:
        mine = run(
            functools.partial(sum_kernel, after=len(after)), part,
            [], mine, swap(mine, "rhs", bit), after=after, name="sum_layers",
        )
        bit, after = 2 * bit, []
    next_layer = swap(mine, "rhs", 1)

    distant_parts = [across_chips(mine, j) for j in distant]
    if len(distant) > 1:
        handed = [swap(run(stack_kernel, bundle, [], *distant_parts, name="stack_distant"), "rhs", 1)]
    else:
        handed = [swap(t, "rhs", 1) for t in distant_parts]

    def spread(value):
        return [value] + [across_direct(value, i) for i in range(1, len(direct))]

    joined = shaped((chips, *part.shape))
    near = run(join_kernel, joined, [], *spread(mine), *distant_parts, name="join_near")
    new_right, done_right = run(
        right_update_kernel, [shaped((w, rows)), done],
        [], right, right_sum, unit, p_high, p_low,
        after=[near], size=0, name="right_update",
    )
    far = run(
        functools.partial(join_kernel, after=1), joined, [], *spread(next_layer), *handed, after=[done_right], name="join_far",
    )
    other_near, other_far = across_cores(near), across_cores(far)
    scratch = [
        pltpu.VMEM((packed, LANES), F32), pltpu.VMEM(operators.shape[1:], F32), pltpu.SemaphoreType.DMA((2,)),
    ]
    half_done = run(
        functools.partial(operator_kernel, own=True), shaped(operators.shape), [], operators, column, near, far,
        scratch=scratch, out_specs=HBM, name="own_operator",
    )
    new_operators = run(
        functools.partial(operator_kernel, own=False), shaped(operators.shape),
        [], operators, column, other_near, other_far, half_done,
        scratch=scratch, out_specs=HBM, in_place=True, name="operator_update",
    )
    return (
        jnp.swapaxes(new_left, 0, 1)[None, None],
        jnp.swapaxes(new_right, 0, 1)[None, None],
        new_operators,
    )


def solution(mesh):
    return jax.shard_map(
        body,
        mesh=mesh,
        in_specs=(
            P("lhs", "rhs", None, None),
            P("lhs", "rhs", None),
            P("lhs", "rhs", None, None),
            P("lhs", "rhs", None),
            P(),
            P(),
            P("lhs", "rhs", None),
            P("lhs", "rhs", None),
            P("lhs", "rhs", None),
            P("lhs", "rhs", None),
            P("lhs", "rhs"),
        ),
        out_specs=(P("lhs", "rhs", None, None), P("lhs", "rhs", None, None), P()),
        check_vma=False,
    )
```

```python
import functools

import jax
import jax.numpy as jnp
from jax import lax
from jax.experimental import pallas as pl
from jax.experimental.pallas import tpu as pltpu
from jax.sharding import PartitionSpec as P

F32 = jnp.float32
BF16 = jnp.bfloat16
LANES = 128
BLOCKS = 4
NN = ((1,), (0,))
NT = ((1,), (1,))
TN = ((0,), (0,))
EPS = 1e-06


def cut(x):
    high = x.astype(BF16)
    low = (x - high.astype(F32)).astype(BF16)
    return high, low


def mul(a, b, dims):
    return lax.dot_general(a, b, (dims, ((), ())), preferred_element_type=F32)


def mul3(a, b, dims):
    return mul(a[0], b[0], dims) + (mul(a[0], b[1], dims) + mul(a[1], b[0], dims))


def deep3(a, b, dims):
    (da,), (db,) = dims
    left = jnp.concatenate([a[0], a[0], a[1]], axis=da)
    right = jnp.concatenate([b[0], b[1], b[0]], axis=db)
    return mul(left, right, dims)


def one_hot(index_row, rows):
    shape = (rows, index_row.shape[1])
    return lax.broadcasted_iota(jnp.int32, shape, 0) == index_row


def prepare_kernel(
    count, src, tgt, neg, ops, op_sums,
    pick, weight, hit, live, column, ops_high, ops_low,
):
    rows, slots = pick.shape
    w = ops.shape[1]
    pick[...] = one_hot(src[...], rows).astype(BF16)
    target = jnp.transpose(one_hot(tgt[...], rows).astype(F32))
    sample = jnp.transpose(one_hot(neg[...], rows).astype(F32))
    alive = (lax.broadcasted_iota(jnp.int32, (slots, 1), 0) < count[0, 0]).astype(F32)
    weight[...] = target + jnp.sum(sample, axis=0, keepdims=True)
    hit[...] = target * alive
    live[...] = alive
    diagonal = one_hot(lax.broadcasted_iota(jnp.int32, (1, w), 1), w)
    for i in range(ops.shape[0]):
        column[i] = jnp.sum(jnp.where(diagonal, op_sums[i:i + 1, :], 0.0), axis=1, keepdims=True)
        high, low = cut(ops[i])
        ops_high[i] = high
        ops_low[i] = low


def left_kernel(after, left, ops_high, ops_low, pick, rel, x_high, x_low, unit, scale, turned):
    high, low = cut(left[...])
    xh = mul(high, pick[...], NN).astype(BF16)
    xl = mul(low, pick[...], NN).astype(BF16)
    x_high[...] = xh
    x_low[...] = xl
    first = mul3((ops_high[0], ops_low[0]), (xh, xl), TN)
    second = mul3((ops_high[1], ops_low[1]), (xh, xl), TN)
    mapped = jnp.where(rel[...] == 0, first, second)
    inv = lax.rsqrt(jnp.sum(mapped * mapped, axis=0, keepdims=True) + EPS)
    u = mapped * inv
    unit[...] = u
    scale[...] = inv
    high, low = cut(jnp.transpose(u))
    turned[...] = jnp.concatenate([high, high, low], axis=1)


def operator_grad(which, relations, d_high, d_low, x, out):
    own = relations == which
    masked = [jnp.where(own, part.astype(F32), 0.0).astype(BF16) for part in (d_high, d_low)]
    grad = deep3(x, masked, NT)
    w = grad.shape[0]
    tiles, rest = w // LANES, w % LANES
    for t in range(tiles):
        out[pl.ds(t * w, w), :] = grad[:, t * LANES:(t + 1) * LANES]
    tail = jnp.transpose(grad[:, tiles * LANES:])
    base = tiles * w
    out[pl.ds(base, out.shape[0] - base), :] = jnp.zeros((out.shape[0] - base, LANES), F32)
    for t in range(-(-w // LANES)):
        width = min(LANES, w - t * LANES)
        out[pl.ds(base + t * rest, rest), 0:width] = tail[:, t * LANES:t * LANES + width]


def right_kernel(
    after, right, unit, scale, turned, weight, hit, live, rel, x_high, x_low,
    send, d_high, d_low, pushes,
):
    r = right[...]
    split = cut(r)
    inv = lax.rsqrt(jnp.sum(r * r, axis=0, keepdims=True) + EPS)
    scores = mul(turned[...], jnp.concatenate([split[0], split[1], split[0]], axis=0), NN) * inv
    weighted = jnp.exp(scores) * weight[...]
    total = jnp.sum(weighted, axis=1, keepdims=True)
    push = weighted * (live[...] / total) - hit[...]
    pushes[...] = push
    du = deep3(split, cut(push * inv), NT)
    u = unit[...]
    along = jnp.sum(u * du, axis=0, keepdims=True)
    dh, dl = cut(scale[...] * (du - u * along))
    d_high[...] = dh
    d_low[...] = dl
    operator_grad(1 - core(), rel[...], dh, dl, (x_high[...], x_low[...]), send)


def keep_kernel(rel, d_high, d_low, x_high, x_low, keep):
    operator_grad(core(), rel[...], d_high[...], d_low[...], (x_high[...], x_low[...]), keep)


def adagrad_t(weights, sums, grad):
    summed = sums + jnp.sum(grad * grad, axis=0, keepdims=True) / grad.shape[0]
    return weights - grad * (0.1 / jnp.sqrt(summed))


def left_update_kernel(
    after, left, left_sum, ops_high, ops_low, pick, rel, d_high, d_low, new_left, done,
):
    d = (d_high[...], d_low[...])
    first = mul3((ops_high[0], ops_low[0]), d, NN)
    second = mul3((ops_high[1], ops_low[1]), d, NN)
    dx = cut(jnp.where(rel[...] == 0, first, second))
    grad = mul(dx[0], pick[...], NT) + mul(dx[1], pick[...], NT)
    new_left[...] = adagrad_t(left[...], left_sum[...], grad)
    done[...] = jnp.zeros_like(done)


def right_update_kernel(after, right, right_sum, unit, pushes, new_right, done):
    r = right[...]
    inv = lax.rsqrt(jnp.sum(r * r, axis=0, keepdims=True) + EPS)
    v = r * inv
    dv = deep3(cut(unit[...]), cut(pushes[...]), NN)
    grad = inv * (dv - v * jnp.sum(v * dv, axis=0, keepdims=True))
    new_right[...] = adagrad_t(r, right_sum[...], grad)
    done[...] = jnp.zeros_like(done)


def core():
    return lax.rem(lax.axis_index("lhs"), 2)


def chip():
    return lax.div(lax.axis_index("lhs"), 2)


def side():
    return lax.rem(lax.axis_index("rhs"), 2)


def by_core(direct):
    first = core() == 0
    return [0] + [jnp.where(first, a, b) for a, b in zip(direct[1:], direct[:0:-1])]


def deal_kernel(one, two, *outs):
    direct, distant = peers_of(one.shape[0])
    for half, own in enumerate((1 - side(), side())):
        own_outs = outs[half * (len(direct) + 1):]

        def part(j):
            spot = jnp.bitwise_xor(chip(), j)
            return one[spot, own] + two[spot, own]

        for j, out in zip(by_core(direct), own_outs):
            out[...] = part(j)
        for i, j in enumerate(distant):
            own_outs[len(direct)][i] = part(j)


def merge_kernel(one, two, *outs):
    for i, out in enumerate(outs):
        out[...] = one[i] + two[i]


def sum_kernel(*refs, after):
    refs = refs[after:]
    refs[-1][...] = functools.reduce(jnp.add, [ref[...] for ref in refs[:-1]])


def join_kernel(*refs, after=0):
    out = refs[-1]
    direct, distant = peers_of(out.shape[0])
    rest = refs[after + len(direct):-1]
    for j, ref in zip(by_core(direct), refs[after:]):
        out[jnp.bitwise_xor(chip(), j)] = ref[...]
    for i, j in enumerate(distant):
        out[jnp.bitwise_xor(chip(), j)] = rest[0][i] if len(rest[0].shape) == 3 else rest[i][...]


def stack_kernel(*refs):
    for i, ref in enumerate(refs[:-1]):
        refs[-1][i] = ref[...]


def operator_rows(which, ops, sums, near, far, flat, out, finish):
    chunk = near.shape[1]
    for j in range(near.shape[0]):
        for own, ref in ((side(), near), (1 - side(), far)):
            flat[pl.ds(pl.multiple_of((2 * j + own) * chunk, 8), chunk), :] = ref[j]
    w = ops.shape[1]
    main = w // LANES
    rest = w - main * LANES
    tiles = [flat[pl.ds(t * w, w), :] for t in range(main)]
    tail = jnp.concatenate(
        [flat[pl.ds(main * w + t * rest, rest), :] for t in range(-(-w // LANES))], axis=1
    )
    tail = jnp.transpose(tail)[:w]
    square = jnp.sum(tail * tail, axis=1, keepdims=True)
    square = square + jnp.sum(sum(tile * tile for tile in tiles), axis=1, keepdims=True)
    rate = 0.1 / jnp.sqrt(sums[which] + square / w)
    cuts = [w * i // (8 * BLOCKS) * 8 for i in range(BLOCKS)] + [w]
    for block in [slice(low, high) for low, high in zip(cuts, cuts[1:])]:
        for t, part in enumerate([*tiles, tail]):
            span = slice(t * LANES, min(w, (t + 1) * LANES))
            out[block, span] = ops[which, block, span] - part[block] * rate[block]
        finish(block)


def operator_kernel(ops, sums, near, far, *refs, own):
    out, flat, half, sem = refs[-4:]
    which = core() if own else 1 - core()
    copies = []

    def finish(block):
        target = out.at[which, block, :]
        copies.append(pltpu.make_async_copy(half.at[block, :], target, sem.at[len(copies)]))
        copies[-1].start()

    operator_rows(which, ops, sums, near, far, flat, half, finish)
    for copy in copies:
        copy.wait()


def shaped(shape, dtype=F32):
    return jax.ShapeDtypeStruct(shape, dtype)


VMEM = pl.BlockSpec(memory_space=pltpu.VMEM)
ANY = pl.BlockSpec(memory_space=pl.ANY)
HBM = pl.BlockSpec(memory_space=pltpu.HBM)
SMEM = pl.BlockSpec(memory_space=pltpu.SMEM)


def run(kernel, out_shape, scalars, *args, after=(), scratch=(), out_specs=None, in_place=False, flops=0, size=2**20, name=None):
    specs = [SMEM] * len(scalars) + [ANY] * len(after) + [VMEM] * len(args)
    if in_place:
        specs[-1] = HBM
    return pl.pallas_call(
        kernel,
        out_shape=out_shape,
        in_specs=specs,
        out_specs=out_specs or jax.tree.map(lambda _: VMEM, out_shape),
        scratch_shapes=scratch,
        input_output_aliases={len(specs) - 1: 0} if in_place else {},
        compiler_params=pltpu.CompilerParams(vmem_limit_bytes=24 * 2**20),
        cost_estimate=pl.CostEstimate(flops=flops, bytes_accessed=size, transcendentals=0),
        name=name,
    )(*scalars, *after, *args)


def around(value, axis, steps):
    count = lax.axis_size(axis)
    return lax.ppermute(value, axis, [(i, (i + steps) % count) for i in range(count)])


def swap(value, axis, bit):
    count = lax.axis_size(axis)
    return lax.ppermute(value, axis, [(i, i ^ bit) for i in range(count)])


def across_cores(value):
    return swap(value, "lhs", 1)


def peers_of(count):
    return [j for j in range(count) if j.bit_count() < 2], [j for j in range(count) if j.bit_count() > 1]


def across_chips(value, j):
    return swap(value, "lhs", 2 * j)


def across_direct(value, spot):
    count = lax.axis_size("lhs")
    direct = peers_of(count // 2)[0]
    return lax.ppermute(value, "lhs", [(i, i ^ (2 * direct[spot if i % 2 == 0 else -spot])) for i in range(count)])


def body(
    left_table, left_state, right_table, right_state, operators, operator_state,
    sources, targets, relations, negatives, counts,
):
    rows, w = left_table.shape[2:]
    slots = sources.shape[2]
    chips = lax.axis_size("lhs") // 2
    layers = lax.axis_size("rhs")
    unit_rows = 16 * chips
    used = w // LANES * w + (w % LANES) * -(-w // LANES)
    packed = -(-used // unit_rows) * unit_rows

    right = around(jnp.swapaxes(right_table[0, 0], 0, 1), "rhs", 1)
    left = around(jnp.swapaxes(left_table[0, 0], 0, 1), "lhs", 1)
    left_sum = around(left_state[0], "lhs", 1)
    right_sum = around(right_state[0], "rhs", 1)
    rel = relations[0]
    wide = shaped((w, slots), BF16)
    turned = shaped((slots, 3 * w), BF16)
    cross = shaped((slots, rows))
    halves = shaped(operators.shape, BF16)
    pick, weight, hit, live, column, ops_high, ops_low = run(
        prepare_kernel,
        [shaped((rows, slots), BF16), cross, cross, shaped((slots, 1)), shaped((*operator_state.shape, 1)),
         halves, halves],
        [counts], sources[0], targets[0], negatives[0], operators, operator_state, name="prepare",
    )
    x_high, x_low, unit, scale, turned = run(
        left_kernel,
        [wide, wide, shaped((w, slots)), shaped((1, slots)), turned],
        [], left, ops_high, ops_low, pick, rel, after=[left_sum], flops=2 * 10**9, name="left_side",
    )
    send, d_high, d_low, pushes = run(
        right_kernel,
        [shaped((packed, LANES)), wide, wide, cross],
        [], right, unit, scale, turned, weight, hit, live, rel, x_high, x_low,
        after=[right_sum], flops=3 * 10**9, name="right_side",
    )
    got = across_cores(send)
    keep = run(
        keep_kernel, shaped((packed, LANES)), [], rel, d_high, d_low, x_high, x_low,
        flops=10**9, name="own_relation",
    )

    part = shaped((packed // chips // 2, LANES))
    direct, distant = peers_of(chips)
    bundle = shaped((len(distant), *part.shape))
    dealt = run(
        deal_kernel, ([part] * len(direct) + [bundle]) * 2, [],
        *[t.reshape(chips, 2, *part.shape) for t in (keep, got)], name="sum_cores",
    )
    away, home = dealt[:len(direct)], dealt[len(direct) + 1:-1]
    merged = run(
        merge_kernel, [part] * len(distant), [], dealt[-1], swap(dealt[len(direct)], "rhs", 1), name="merge_layers",
    )
    away = [away[0]] + [across_direct(t, i + 1) for i, t in enumerate(away[1:])]
    home = [home[0]] + [across_direct(t, i + 1) for i, t in enumerate(home[1:])]
    home += [across_chips(t, j) for j, t in zip(distant, merged)]
    passed = run(functools.partial(sum_kernel, after=1), part, [], *away, after=merged[:1], name="sum_away")
    done = shaped((8, LANES))
    mine = run(
        functools.partial(sum_kernel, after=0), part, [], *home, swap(passed, "rhs", 1), name="sum_home",
    )
    new_left, done_left = run(
        left_update_kernel, [shaped((w, rows)), done],
        [], left, left_sum, ops_high, ops_low, pick, rel, d_high, d_low,
        after=[mine], flops=2 * 10**9, name="left_update",
    )
    bit, after = 2, [done_left]
    while bit < layers:
        mine = run(
            functools.partial(sum_kernel, after=len(after)), part,
            [], mine, swap(mine, "rhs", bit), after=after, name="sum_layers",
        )
        bit, after = 2 * bit, []
    next_layer = swap(mine, "rhs", 1)

    distant_parts = [across_chips(mine, j) for j in distant]
    if len(distant) > 1:
        handed = [swap(run(stack_kernel, bundle, [], *distant_parts, name="stack_distant"), "rhs", 1)]
    else:
        handed = [swap(t, "rhs", 1) for t in distant_parts]

    def spread(value):
        return [value] + [across_direct(value, i) for i in range(1, len(direct))]

    joined = shaped((chips, *part.shape))
    near = run(join_kernel, joined, [], *spread(mine), *distant_parts, name="join_near")
    new_right, done_right = run(
        right_update_kernel, [shaped((w, rows)), done],
        [], right, right_sum, unit, pushes,
        after=[near], size=0, name="right_update",
    )
    far = run(
        functools.partial(join_kernel, after=1), joined, [], *spread(next_layer), *handed, after=[done_right], name="join_far",
    )
    other_near, other_far = across_cores(near), across_cores(far)
    scratch = [
        pltpu.VMEM((packed, LANES), F32), pltpu.VMEM(operators.shape[1:], F32), pltpu.SemaphoreType.DMA((BLOCKS,)),
    ]
    half_done = run(
        functools.partial(operator_kernel, own=True), shaped(operators.shape), [], operators, column, near, far,
        scratch=scratch, out_specs=HBM, name="own_operator",
    )
    new_operators = run(
        functools.partial(operator_kernel, own=False), shaped(operators.shape),
        [], operators, column, other_near, other_far, half_done,
        scratch=scratch, out_specs=HBM, in_place=True, name="operator_update",
    )
    return (
        jnp.swapaxes(new_left, 0, 1)[None, None],
        jnp.swapaxes(new_right, 0, 1)[None, None],
        new_operators,
    )


def solution(mesh):
    return jax.shard_map(
        body,
        mesh=mesh,
        in_specs=(
            P("lhs", "rhs", None, None),
            P("lhs", "rhs", None),
            P("lhs", "rhs", None, None),
            P("lhs", "rhs", None),
            P(),
            P(),
            P("lhs", "rhs", None),
            P("lhs", "rhs", None),
            P("lhs", "rhs", None),
            P("lhs", "rhs", None),
            P("lhs", "rhs"),
        ),
        out_specs=(P("lhs", "rhs", None, None), P("lhs", "rhs", None, None), P()),
        check_vma=False,
    )
```
